32 devices in a mesh: parts: 2 (over y), band: 4 (over z), feat: 2 (over x), rep: 2 (over core).
Axes of the slice: x: 2, y: 2, z: 4, core: 2. Of those that a mesh axis runs over, the one named last changes fastest.
Arguments:
- grid_in: bfloat16 [8192, 520], P(('parts', 'band', 'feat', 'rep')), parts along dimension 0, may hold values from -6 to 6
- target: bfloat16 [8192, 520], P(('parts', 'band', 'feat', 'rep')), parts along dimension 0, may hold values from -6 to 6
- mesh_in: bfloat16 [4096, 512], P(('parts', 'band', 'feat', 'rep')), parts along dimension 0, may hold values from -6 to 6
- embed_weight: bfloat16 [520, 512], P(None, 'feat'), may hold values from -0.25 to 0.25
- encode_project: bfloat16 [512, 512], P(None, 'feat'), may hold values from -0.25 to 0.25
- encode_attr_weight: bfloat16 [4, 512], replicated, may hold values from -3 to 3
- encode_edge_weight: bfloat16 [512, 512], P(None, 'feat'), may hold values from -0.25 to 0.25
- node_weight: bfloat16 [512, 512], P(None, 'feat'), may hold values from -0.25 to 0.25
- node_gain: bfloat16 [512], replicated, may hold values from 0.099609375 to 1.8984375
- decode_project: bfloat16 [512, 512], P(None, 'feat'), may hold values from -0.25 to 0.25
- decode_attr_weight: bfloat16 [4, 512], replicated, may hold values from -3 to 3
- decode_edge_weight: bfloat16 [512, 512], P(None, 'feat'), may hold values from -0.25 to 0.25
- out_weight: bfloat16 [512, 520], replicated, may hold values from -0.25 to 0.25
- encode_senders: int32 [32, 4, 32], P(('parts', 'band', 'feat', 'rep')), parts along dimension 0, may hold values from 0 to 255, as said below
- encode_receivers: int32 [32, 4, 32], P(('parts', 'band', 'feat', 'rep')), parts along dimension 0, may hold values from -1 to 127, as said below
- encode_features: bfloat16 [32, 4, 128], P(('parts', 'band', 'feat', 'rep')), parts along dimension 0, may hold values from -6 to 6
- decode_senders: int32 [32, 4, 64], P(('parts', 'band', 'feat', 'rep')), parts along dimension 0, may hold values from 0 to 127, as said below
- decode_receivers: int32 [32, 4, 64], P(('parts', 'band', 'feat', 'rep')), parts along dimension 0, may hold values from -1 to 255, as said below
- decode_features: bfloat16 [32, 4, 256], P(('parts', 'band', 'feat', 'rep')), parts along dimension 0, may hold values from -6 to 6
Outputs:
- predicted: bfloat16 [8192, 520], P(('parts', 'band', 'feat', 'rep')), parts along dimension 0
- edge_gradient: float32 [1024, 512], P('parts', 'feat'), parts along dimension 0
The draws below stay inside these ranges and needn't reach their ends.
There are 2 independent parts, one for each index of `parts`. The reference program is written for one: setup_inputs(seed, part) draws one part's arguments, and reference() takes and returns one part's arrays. A program takes and returns all parts, laid end to end along the dimension named above; an argument that names none is the same for every part. Nothing has to cross between parts.
Inputs may be any that keep to these rules, and one draw needn't show every extreme that they name: encode_senders[k, p, c] is a row within the 256 grid points of slab k. encode_receivers[j, b, c] is a row within the 128 mesh nodes of slab j, or -1 for an empty slot. The used slots of a block come first. A block from band b to partition p is empty when p and b differ by more than 2; it uses 1 to 16 slots when they differ by at most 1, and 1 to 8 when they differ by 2. For one partition, drawn from the seed, every block bound to it from a band within 2 of it is full (32 slots). decode_senders[j, b, c] is a row within the 128 mesh nodes of slab j. decode_receivers[k, p, c] is a row within the 256 grid points of slab k, or -1 for an empty slot. The used slots of a block come first. A block from partition p to band b is empty when p and b differ by more than 2; it uses 1 to 32 slots when they differ by at most 1, and 1 to 16 when they differ by 2. For one band, drawn from the seed, every block bound to it from a partition within 2 of it is full (64 slots).
All inputs are finite; a program needn't handle non-finite values.
Results may differ from the reference program's by a relative error of at most 0.0075.
Values may be sent and summed in bfloat16 or wider, within the bound.
A program may use at most 64 MiB of HBM per device.

```python
import math
import jax
import jax.numpy as jnp
from jax import lax

WIDTH = 512
VALUES = 520
ATTRS = 4
GRID_DEV = 256
MESH_DEV = 128
CAP_ENC = 32
CAP_DEC = 64
SLABS = 16
GRID = 4096
MESH = 2048
N_BAND = 4
N_FEAT = 2
N_REP = 2


def edge_blocks(key, capacity, source_high, target_high):
    subs_count = N_FEAT * N_REP
    slab_count = N_BAND * subs_count
    hot_key, near_key, far_key, source_key, target_key = jax.random.split(key, 5)
    hot_part = jax.random.randint(hot_key, (), 0, N_BAND)
    band_of = (jnp.arange(slab_count) // subs_count)[:, None]
    partition = jnp.arange(N_BAND)[None, :]
    distance = jnp.abs(partition - band_of)
    near_counts = jax.random.randint(near_key, (slab_count, N_BAND), 1, capacity // 2 + 1)
    far_counts = jax.random.randint(far_key, (slab_count, N_BAND), 1, max(1, capacity // 4) + 1)
    counts = jnp.where(distance <= 1, near_counts, jnp.where(distance == 2, far_counts, 0))
    counts = jnp.where((partition == hot_part) & (distance <= 2), capacity, counts)
    slot_index = jnp.arange(capacity)[None, None, :]
    is_live = slot_index < counts[:, :, None]
    sources = jax.random.randint(source_key, (slab_count, N_BAND, capacity), 0, source_high)
    targets = jnp.where(is_live, jax.random.randint(target_key, (slab_count, N_BAND, capacity), 0, target_high), -1)
    arranged = targets.reshape(N_BAND, subs_count, N_BAND, capacity).transpose(2, 1, 0, 3).reshape(slab_count, N_BAND, capacity)
    return (sources.astype(jnp.int32), arranged.astype(jnp.int32))


def draw_encode_senders(key, part):
    senders, receivers = edge_blocks(jax.random.fold_in(key, 11), CAP_ENC, GRID_DEV, MESH_DEV)
    return senders


def draw_encode_receivers(key, part):
    senders, receivers = edge_blocks(jax.random.fold_in(key, 11), CAP_ENC, GRID_DEV, MESH_DEV)
    return receivers


def draw_decode_senders(key, part):
    senders, receivers = edge_blocks(jax.random.fold_in(key, 12), CAP_DEC, MESH_DEV, GRID_DEV)
    return senders


def draw_decode_receivers(key, part):
    senders, receivers = edge_blocks(jax.random.fold_in(key, 12), CAP_DEC, MESH_DEV, GRID_DEV)
    return receivers


def block_scale(own_key, dims, pieces, least, largest):
    def one(axis_at, shards_of):
        steps = jax.random.uniform(jax.random.fold_in(jax.random.fold_in(own_key, 6), axis_at), (shards_of,), jnp.float32, least / len(pieces), largest / len(pieces))
        return jnp.repeat(jnp.exp(steps), dims[axis_at] // shards_of).reshape((-1,) + (1,) * (len(dims) - axis_at - 1))

    factor_of = one(*pieces[0])
    for cut in pieces[1:]:
        factor_of = factor_of * one(*cut)
    return factor_of


def noise(own_key, extent, scale, limit, cuts=(), kind=jnp.bfloat16):
    gain = block_scale(own_key, extent, cuts, -0.22, 0.18) if cuts else 1.0
    drawn = jax.random.normal(own_key, extent, jnp.float32) * scale * gain
    return jnp.minimum(jnp.maximum(drawn, -limit), limit).astype(kind)


def setup_inputs(seed: int = 0, part: int = 0) -> dict:
    splits = jax.random.split(jax.random.key(seed), 20)
    part_splits = jax.random.split(jax.random.fold_in(splits[19], part), 20)
    grid_in = noise(part_splits[0], (GRID, VALUES), 1.0, 6.0, ((0, 16),))
    target = noise(part_splits[1], (GRID, VALUES), 1.0, 6.0, ((0, 16),))
    mesh_in = noise(part_splits[2], (MESH, WIDTH), 1.0, 6.0, ((0, 16),))
    embed_weight = noise(splits[3], (VALUES, WIDTH), VALUES ** -0.5, 0.25, ((1, 2),))
    encode_project = noise(splits[4], (WIDTH, WIDTH), WIDTH ** -0.5, 0.25, ((1, 2),))
    encode_attr_weight = noise(splits[5], (ATTRS, WIDTH), ATTRS ** -0.5, 3.0)
    encode_edge_weight = noise(splits[6], (WIDTH, WIDTH), WIDTH ** -0.5, 0.25, ((1, 2),))
    node_weight = noise(splits[7], (WIDTH, WIDTH), WIDTH ** -0.5, 0.25, ((1, 2),))
    node_gain = jnp.clip(1.0 + 0.18 * jax.random.normal(splits[8], (WIDTH,), jnp.float32), 0.099609375, 1.8984375).astype(jnp.bfloat16)
    decode_project = noise(splits[9], (WIDTH, WIDTH), WIDTH ** -0.5, 0.25, ((1, 2),))
    decode_attr_weight = noise(splits[10], (ATTRS, WIDTH), ATTRS ** -0.5, 3.0)
    decode_edge_weight = noise(splits[11], (WIDTH, WIDTH), WIDTH ** -0.5, 0.25, ((1, 2),))
    out_weight = noise(splits[12], (WIDTH, VALUES), WIDTH ** -0.5, 0.25)
    encode_senders = draw_encode_senders(jax.random.fold_in(jax.random.fold_in(splits[19], part), 71), part)
    encode_receivers = draw_encode_receivers(jax.random.fold_in(jax.random.fold_in(splits[19], part), 71), part)
    encode_features = noise(part_splits[15], (SLABS, ATTRS, N_BAND * CAP_ENC), 1.0, 6.0, ((0, 16),))
    decode_senders = draw_decode_senders(jax.random.fold_in(jax.random.fold_in(splits[19], part), 71), part)
    decode_receivers = draw_decode_receivers(jax.random.fold_in(jax.random.fold_in(splits[19], part), 71), part)
    decode_features = noise(part_splits[18], (SLABS, ATTRS, N_BAND * CAP_DEC), 1.0, 6.0, ((0, 16),))
    return {"grid_in": grid_in, "target": target, "mesh_in": mesh_in, "embed_weight": embed_weight, "encode_project": encode_project, "encode_attr_weight": encode_attr_weight, "encode_edge_weight": encode_edge_weight, "node_weight": node_weight, "node_gain": node_gain, "decode_project": decode_project, "decode_attr_weight": decode_attr_weight, "decode_edge_weight": decode_edge_weight, "out_weight": out_weight, "encode_senders": encode_senders, "encode_receivers": encode_receivers, "encode_features": encode_features, "decode_senders": decode_senders, "decode_receivers": decode_receivers, "decode_features": decode_features}


eps_norm = 1e-05

def edge_act(node_table, source_rows, features, attr_weight):
    picked = jnp.take(node_table, source_rows, axis=0).astype(jnp.float32)
    attr_term = jnp.einsum('cs,cd->sd', features.astype(jnp.float32), attr_weight.astype(jnp.float32))
    return jax.nn.silu(picked + attr_term).astype(jnp.bfloat16)

def edge_layout(senders, receivers, slab_index, own_rows, peer_rows):
    subs_count = N_FEAT * N_REP
    band_index = slab_index // subs_count
    sub_index = slab_index % subs_count
    peer_slab = jnp.arange(N_BAND, dtype=jnp.int32) * subs_count + sub_index
    local_rows = receivers[peer_slab, band_index]
    source_rows = slab_index * own_rows + senders[slab_index].reshape(-1)
    is_live = (local_rows >= 0).reshape(-1)
    target_rows = (peer_slab[:, None] * peer_rows + local_rows).reshape(-1)
    return (source_rows, is_live, target_rows)

def reference(grid_in, target, mesh_in, embed_weight, encode_project, encode_attr_weight, encode_edge_weight, node_weight, node_gain, decode_project, decode_attr_weight, decode_edge_weight, out_weight, encode_senders, encode_receivers, encode_features, decode_senders, decode_receivers, decode_features):
    grid_latent = jax.nn.silu(jnp.dot(grid_in, embed_weight, preferred_element_type=jnp.float32)).astype(jnp.bfloat16)
    grid_project = jnp.dot(grid_latent, encode_project, preferred_element_type=jnp.float32).astype(jnp.bfloat16)
    slab_list = jnp.arange(SLABS, dtype=jnp.int32)

    def encode_step(running, slab_index):
        source_rows, is_live, target_rows = edge_layout(encode_senders, encode_receivers, slab_index, GRID_DEV, MESH_DEV)
        act_rows = edge_act(grid_project, source_rows, encode_features[slab_index], encode_attr_weight)
        message = jnp.dot(act_rows, encode_edge_weight, preferred_element_type=jnp.float32).astype(jnp.bfloat16)
        target_rows = jnp.where(is_live, target_rows, MESH)
        return (running.at[target_rows].add(message.astype(jnp.float32), mode='drop'), None)
    summed, unused = lax.scan(encode_step, jnp.zeros((MESH, WIDTH), jnp.float32), slab_list)
    aggregated = summed.astype(jnp.bfloat16)
    update = mesh_in.astype(jnp.float32) + jnp.dot(aggregated, node_weight, preferred_element_type=jnp.float32)
    centre = lax.optimization_barrier(jnp.mean(update, axis=-1, keepdims=True))
    centered = update - centre
    spread = lax.optimization_barrier(jnp.mean(centered * centered, axis=-1, keepdims=True))
    mesh_latent = (node_gain.astype(jnp.float32) * centered * lax.rsqrt(spread + eps_norm)).astype(jnp.bfloat16)
    mesh_project = jnp.dot(mesh_latent, decode_project, preferred_element_type=jnp.float32).astype(jnp.bfloat16)

    def decode_step(running, slab_index):
        source_rows, is_live, target_rows = edge_layout(decode_senders, decode_receivers, slab_index, MESH_DEV, GRID_DEV)
        act_rows = edge_act(mesh_project, source_rows, decode_features[slab_index], decode_attr_weight)
        message = jnp.dot(act_rows, decode_edge_weight, preferred_element_type=jnp.float32).astype(jnp.bfloat16)
        target_rows = jnp.where(is_live, target_rows, GRID)
        return (running.at[target_rows].add(message.astype(jnp.float32), mode='drop'), None)
    incoming, unused = lax.scan(decode_step, jnp.zeros((GRID, WIDTH), jnp.float32), slab_list)
    decoded = (grid_latent.astype(jnp.float32) + incoming).astype(jnp.bfloat16)
    predicted = jnp.dot(decoded, out_weight, preferred_element_type=jnp.float32).astype(jnp.bfloat16)
    error = ((predicted.astype(jnp.float32) - target.astype(jnp.float32)) / math.sqrt(GRID)).astype(jnp.bfloat16)
    grid_cotangent = jnp.dot(error, out_weight.T, preferred_element_type=jnp.float32).astype(jnp.bfloat16)

    def gradient_step(running, slab_index):
        source_rows, is_live, target_rows = edge_layout(decode_senders, decode_receivers, slab_index, MESH_DEV, GRID_DEV)
        act_rows = edge_act(mesh_project, source_rows, decode_features[slab_index], decode_attr_weight)
        safe_rows = jnp.where(is_live, target_rows, 0)
        cotangent = jnp.where(is_live[:, None], jnp.take(grid_cotangent, safe_rows, axis=0), jnp.zeros((), jnp.bfloat16))
        return (running + jnp.dot(act_rows.T, cotangent, preferred_element_type=jnp.float32), None)
    edge_gradient, unused = lax.scan(gradient_step, jnp.zeros((WIDTH, WIDTH), jnp.float32), slab_list)
    return (predicted, edge_gradient)
```

```python
import functools
import math

import jax
import jax.numpy as jnp
from jax import lax
from jax.experimental import pallas as pl
from jax.experimental.pallas import tpu as pltpu
from jax.sharding import PartitionSpec as P

eps_norm = 1e-05
MESH = pl.DeviceIdType.MESH
F32 = jnp.float32
BF16 = jnp.bfloat16
REACH = 2
HOPS = tuple(d for d in range(-REACH, REACH + 1) if d != 0)


def silu(v):
    return v / (1.0 + jnp.exp(-v))


def matmul(a, b):
    return jnp.dot(a, b, preferred_element_type=F32)


def matmul_tn(a, b):
    return lax.dot_general(a, b, (((0,), (0,)), ((), ())), preferred_element_type=F32)


def matmul_nt(a, b):
    return lax.dot_general(a, b, (((1,), (1,)), ((), ())), preferred_element_type=F32)


def onehot_rows(index_row, rows):
    at = lax.broadcasted_iota(jnp.int32, (rows, index_row.shape[1]), 0)
    return jnp.where(at == index_row, 1.0, 0.0).astype(BF16)


def forecaster(
    sizes,
    grid_in,
    target,
    mesh_in,
    embed_weight,
    encode_project,
    encode_attr_weight,
    encode_edge_weight,
    node_weight,
    node_gain,
    decode_project,
    decode_attr_weight,
    decode_edge_weight,
    out_weight,
    encode_senders,
    encode_receivers,
    encode_features,
    decode_senders,
    decode_receivers,
    decode_features,
    predicted_ref,
    gradient_ref,
    embed_full,
    weights_full,
    latent,
    encode_out,
    encode_in,
    decode_out,
    decode_in,
    collected,
    half_out,
    half_in,
    mine,
    pieces_out,
    pieces_in,
    final_out,
    final_in,
    w_send,
    w_recv,
    f_send,
    f_recv,
    e_send,
    e_recv,
    d_send,
    d_recv,
    h_sem,
    p_send,
    p_recv,
    g_send,
    g_recv,
):
    nb, nf, inside = sizes
    band, feat, rep = lax.axis_index("band"), lax.axis_index("feat"), lax.axis_index("rep")
    other = 1 - rep
    width = mesh_in.shape[1]
    columns = width // nf
    grid_rows, values = grid_in.shape
    mesh_rows = mesh_in.shape[0]
    group = nb * nf
    lane = nb * 2

    def in_range(b):
        return jnp.logical_and(b >= 0, b < nb)

    encode_in[...] = jnp.zeros_like(encode_in)
    decode_in[...] = jnp.zeros_like(decode_in)
    own = pl.ds(pl.multiple_of(feat * columns, columns), columns)
    padded = embed_full.shape[0]
    embed_full[pl.ds(padded - 32, 32), own] = jnp.zeros((32, columns), BF16)
    embed_full[pl.ds(0, values), own] = embed_weight[...]

    barrier = pltpu.get_barrier_semaphore()
    if inside:
        for db in range(nb):
            for df in range(nf):
                for dr in range(2):
                    if db + df + dr:
                        pl.semaphore_signal(
                            barrier,
                            inc=1,
                            device_id={
                                "band": lax.rem(band + db, nb),
                                "feat": lax.rem(feat + df, nf),
                                "rep": lax.rem(rep + dr, 2),
                            },
                            device_id_type=MESH,
                        )
    else:
        pl.semaphore_signal(barrier, inc=1, device_id={"rep": other}, device_id_type=MESH)
        for df in range(1, nf):
            pl.semaphore_signal(
                barrier, inc=1, device_id={"feat": lax.rem(feat + df, nf)}, device_id_type=MESH
            )
        for d in HOPS:
            @pl.when(in_range(band + d))
            def _():
                pl.semaphore_signal(barrier, inc=1, device_id={"band": band + d}, device_id_type=MESH)

    shards = (encode_project, encode_edge_weight, node_weight, decode_project, decode_edge_weight)
    for i, shard in enumerate(shards):
        weights_full[i, :, own] = shard[...]

    if inside:
        pl.semaphore_wait(barrier, group * 2 - 1)
    else:
        pl.semaphore_wait(barrier, nf)
        for d in HOPS:
            @pl.when(in_range(band + d))
            def _():
                pl.semaphore_wait(barrier, 1)

    def part(i, r, f):
        cols = pl.ds(pl.multiple_of(f * columns, columns), columns)
        if i == 0:
            h = padded // 2
            return embed_full.at[pl.ds(pl.multiple_of(r * h, 16), h), cols]
        h = width // 2
        return weights_full.at[i - 1, pl.ds(pl.multiple_of(r * h, 16), h), cols]

    def across(i, off):
        view = part(i, rep, feat)
        return pltpu.make_async_remote_copy(
            src_ref=view,
            dst_ref=view,
            send_sem=w_send.at[i, off - 1],
            recv_sem=w_recv.at[i, off - 1],
            device_id={"feat": lax.rem(feat + off, nf)},
            device_id_type=MESH,
        )

    def handed(i, off):
        view = part(i, rep, lax.rem(feat + nf - off, nf))
        return pltpu.make_async_remote_copy(
            src_ref=view,
            dst_ref=view,
            send_sem=f_send.at[i, off - 1],
            recv_sem=f_recv.at[i, off - 1],
            device_id={"rep": other},
            device_id_type=MESH,
        )

    def hand_on(i):
        for off in range(1, nf):
            across(i, off).wait_recv()
            handed(i, off).start()

    def ready(i):
        for off in range(1, nf):
            handed(i, off).wait_recv()

    for i in range(6):
        for off in range(1, nf):
            across(i, off).start()

    def message(out, arrive, send_sem, recv_sem, cap, k):
        return pltpu.make_async_remote_copy(
            src_ref=out.at[pl.ds(pl.multiple_of((band + HOPS[k]) * cap, cap), cap)],
            dst_ref=arrive.at[pl.ds(pl.multiple_of(band * cap, cap), cap)],
            send_sem=send_sem.at[k],
            recv_sem=recv_sem.at[k],
            device_id={"band": band + HOPS[k]},
            device_id_type=MESH,
        )

    def send_all(out, arrive, send_sem, recv_sem, cap):
        for k, d in enumerate(HOPS):
            @pl.when(in_range(band + d))
            def _():
                message(out, arrive, send_sem, recv_sem, cap, k).start()
        here = pl.ds(pl.multiple_of(band * cap, cap), cap)
        arrive[here, :] = out[here, :]

    def recv_all(out, arrive, send_sem, recv_sem, cap):
        for k, d in enumerate(HOPS):
            @pl.when(in_range(band - d))
            def _():
                pltpu.make_async_remote_copy(
                    src_ref=out.at[pl.ds(0, cap)],
                    dst_ref=arrive.at[pl.ds(pl.multiple_of((band - d) * cap, cap), cap)],
                    send_sem=send_sem.at[k],
                    recv_sem=recv_sem.at[k],
                    device_id={"band": band - d},
                    device_id_type=MESH,
                ).wait_recv()

    def sent_all(out, arrive, send_sem, recv_sem, cap):
        for k, d in enumerate(HOPS):
            @pl.when(in_range(band + d))
            def _():
                message(out, arrive, send_sem, recv_sem, cap, k).wait_send()

    cap_e = encode_out.shape[0] // nb
    cap_d = decode_out.shape[0] // nb
    enc = (encode_out, encode_in, e_send, e_recv, cap_e)
    dec = (decode_out, decode_in, d_send, d_recv, cap_d)

    encode_attr = matmul_tn(encode_features[0], encode_attr_weight[...])
    encode_pick = onehot_rows(encode_senders[...], grid_rows)
    hand_on(0)
    ready(0)
    latent[...] = silu(matmul(grid_in[...], embed_full[pl.ds(0, values), :])).astype(BF16)
    hand_on(1)
    ready(1)
    grid_project = matmul(latent[...], weights_full[0]).astype(BF16)
    encode_out[...] = silu(matmul_tn(encode_pick, grid_project) + encode_attr).astype(BF16)
    send_all(*enc)

    hand_on(2)
    decode_attr = matmul_tn(decode_features[0], decode_attr_weight[...])
    decode_pick = onehot_rows(decode_senders[...], mesh_rows)
    encode_collect = onehot_rows(encode_receivers[...], mesh_rows)
    decode_collect = onehot_rows(decode_receivers[...], grid_rows)
    recv_all(*enc)
    gathered = matmul(encode_collect, encode_in[...]).astype(BF16)
    ready(2)
    aggregated = matmul(gathered, weights_full[1]).astype(BF16)
    hand_on(3)
    ready(3)
    update = mesh_in[...].astype(F32) + matmul(aggregated, weights_full[2])
    hand_on(4)
    centered = update - jnp.mean(update, axis=-1, keepdims=True)
    spread = jnp.mean(centered * centered, axis=-1, keepdims=True)
    mesh_latent = (node_gain[...].astype(F32) * centered * lax.rsqrt(spread + eps_norm)).astype(BF16)
    ready(4)
    mesh_project = matmul(mesh_latent, weights_full[3]).astype(BF16)
    decode_out[...] = silu(matmul_tn(decode_pick, mesh_project) + decode_attr).astype(BF16)
    send_all(*dec)
    hand_on(5)
    ready(5)
    recv_all(*dec)

    collected[...] = matmul(decode_collect, decode_in[...]).astype(BF16)
    incoming = matmul(collected[...], weights_full[4])
    decoded = (latent[...].astype(F32) + incoming).astype(BF16)
    predicted = matmul(decoded, out_weight[...]).astype(BF16)
    predicted_ref[...] = predicted
    scale = math.sqrt(grid_rows * nb * nf * 2)
    error = ((predicted.astype(F32) - target[...].astype(F32)) / scale).astype(BF16)
    cotangent = matmul_nt(error, out_weight[...]).astype(BF16)

    if not inside:
        gradient_ref[...] = matmul_tn(collected[...], cotangent)
    else:
        half = width // 2
        rows = half // nb

        def term(r):
            return matmul_tn(
                collected[:, pl.ds(pl.multiple_of(r * half, half), half)], cotangent
            )

        half_out[...] = term(other).astype(BF16)
        swap = pltpu.make_async_remote_copy(
            src_ref=half_out,
            dst_ref=half_in,
            send_sem=h_sem.at[0],
            recv_sem=h_sem.at[1],
            device_id={"rep": other},
            device_id_type=MESH,
        )
        swap.start()
        mine[...] = term(rep)
        swap.wait_recv()
        summed = mine[...] + half_in[...].astype(F32)
        mine[...] = summed
        pieces_out[...] = summed.astype(BF16)
        place = band * nf + feat

        def piece(k):
            to = lax.rem(place + k, group)
            tb, tf = lax.div(to, nf), lax.rem(to, nf)
            return pltpu.make_async_remote_copy(
                src_ref=pieces_out.at[
                    pl.ds(pl.multiple_of(tb * rows, 16), rows),
                    pl.ds(pl.multiple_of(tf * columns, columns), columns),
                ],
                dst_ref=pieces_in.at[k - 1],
                send_sem=p_send.at[k - 1],
                recv_sem=p_recv.at[k - 1],
                device_id={"band": tb, "feat": tf},
                device_id_type=MESH,
            )

        for k in range(1, group):
            piece(k).start()
        total = mine[pl.ds(pl.multiple_of(band * rows, 16), rows), own]
        for k in range(1, group):
            piece(k).wait_recv()
            total = total + pieces_in[k - 1].astype(F32)
        final_out[...] = total.astype(BF16)
        spot = band * 2 + rep

        def final(k):
            to = lax.rem(spot + k, lane)
            return pltpu.make_async_remote_copy(
                src_ref=final_out,
                dst_ref=final_in.at[k - 1],
                send_sem=g_send.at[k - 1],
                recv_sem=g_recv.at[k - 1],
                device_id={"band": lax.div(to, 2), "rep": lax.rem(to, 2)},
                device_id_type=MESH,
            )

        def rows_of(s):
            start = lax.rem(s, 2) * half + lax.div(s, 2) * rows
            return pl.ds(pl.multiple_of(start, 16), rows)

        for k in range(1, lane):
            final(k).start()
        gradient_ref[rows_of(spot), :] = final_out[...].astype(F32)
        for k in range(1, lane):
            final(k).wait_recv()
            gradient_ref[rows_of(lax.rem(spot + lane - k, lane)), :] = final_in[k - 1].astype(F32)

    for i in range(6):
        for off in range(1, nf):
            across(i, off).wait_send()
            handed(i, off).wait_send()
    sent_all(*enc)
    sent_all(*dec)
    if inside:
        swap.wait_send()
        for k in range(1, group):
            piece(k).wait_send()
        for k in range(1, lane):
            final(k).wait_send()


def local(sizes, *args):
    nb, nf, inside = sizes
    args = list(args)
    grid_in, mesh_in = args[0], args[2]
    width = mesh_in.shape[1]
    columns = width // nf
    args[8] = args[8].reshape(1, width)
    for at in (13, 14, 16, 17):
        args[at] = args[at].reshape(1, -1)
    cap_e = args[13].shape[1]
    cap_d = args[16].shape[1]
    half = width // 2
    rows = half // nb if inside else 16
    padded = -(-grid_in.shape[1] // 32) * 32
    slots = max(nf - 1, 1)
    dma = pltpu.SemaphoreType.DMA
    group, lane = (nb * nf, nb * 2) if inside else (2, 2)
    predicted, gradient = pl.pallas_call(
        functools.partial(forecaster, sizes),
        out_shape=(
            jax.ShapeDtypeStruct(grid_in.shape, BF16),
            jax.ShapeDtypeStruct((width, columns if inside else width), F32),
        ),
        in_specs=[pl.BlockSpec(memory_space=pltpu.VMEM)] * len(args),
        out_specs=(pl.BlockSpec(memory_space=pltpu.VMEM),) * 2,
        scratch_shapes=[
            pltpu.VMEM((padded, width), BF16),
            pltpu.VMEM((5, width, width), BF16),
            pltpu.VMEM((grid_in.shape[0], width), BF16),
            pltpu.VMEM((cap_e, width), BF16),
            pltpu.VMEM((cap_e, width), BF16),
            pltpu.VMEM((cap_d, width), BF16),
            pltpu.VMEM((cap_d, width), BF16),
            pltpu.VMEM((grid_in.shape[0], width), BF16),
            pltpu.VMEM((half, width), BF16),
            pltpu.VMEM((half, width), BF16),
            pltpu.VMEM((half, width), F32),
            pltpu.VMEM((half, width), BF16),
            pltpu.VMEM((group - 1, rows, columns), BF16),
            pltpu.VMEM((rows, columns), BF16),
            pltpu.VMEM((lane - 1, rows, columns), BF16),
            dma((6, slots)),
            dma((6, slots)),
            dma((6, slots)),
            dma((6, slots)),
            dma((len(HOPS),)),
            dma((len(HOPS),)),
            dma((len(HOPS),)),
            dma((len(HOPS),)),
            dma((2,)),
            dma((group - 1,)),
            dma((group - 1,)),
            dma((lane - 1,)),
            dma((lane - 1,)),
        ],
        compiler_params=pltpu.CompilerParams(
            collective_id=0, has_side_effects=True, vmem_limit_bytes=48 * 1024 * 1024
        ),
    )(*args)
    if not inside:
        total = lax.psum(gradient, ("band", "feat", "rep"))
        gradient = lax.dynamic_slice_in_dim(total, lax.axis_index("feat") * columns, columns, 1)
    return (predicted, gradient)


def solution(mesh):
    nb, nf = mesh.shape["band"], mesh.shape["feat"]
    inside = nb <= 8 and nf <= 2
    slab = ("parts", "band", "feat", "rep")
    return jax.shard_map(
        functools.partial(local, (nb, nf, inside)),
        mesh=mesh,
        in_specs=(
            P(slab, None),
            P(slab, None),
            P(slab, None),
            P(None, "feat"),
            P(None, "feat"),
            P(),
            P(None, "feat"),
            P(None, "feat"),
            P(),
            P(None, "feat"),
            P(),
            P(None, "feat"),
            P(),
        )
        + (P(slab, None, None),) * 6,
        out_specs=(P(slab, None), P("parts", "feat")),
        check_vma=False,
    )
```

```python
import functools
import math

import jax
import jax.numpy as jnp
from jax import lax
from jax.experimental import pallas as pl
from jax.experimental.pallas import tpu as pltpu
from jax.sharding import PartitionSpec as P

eps_norm = 1e-05
MESH = pl.DeviceIdType.MESH
F32 = jnp.float32
BF16 = jnp.bfloat16
REACH = 2
HOPS = tuple(d for d in range(-REACH, REACH + 1) if d != 0)


def silu(v):
    return v / (1.0 + jnp.exp(-v))


def matmul(a, b):
    return jnp.dot(a, b, preferred_element_type=F32)


def matmul_tn(a, b):
    return lax.dot_general(a, b, (((0,), (0,)), ((), ())), preferred_element_type=F32)


def matmul_nt(a, b):
    return lax.dot_general(a, b, (((1,), (1,)), ((), ())), preferred_element_type=F32)


def onehot_rows(index_row, rows):
    at = lax.broadcasted_iota(jnp.int32, (rows, index_row.shape[1]), 0)
    return jnp.where(at == index_row, 1.0, 0.0).astype(BF16)


def forecaster(
    sizes,
    grid_in_hbm,
    target_hbm,
    mesh_in_hbm,
    embed_hbm,
    encode_project_hbm,
    encode_attr_hbm,
    encode_edge_hbm,
    node_weight_hbm,
    node_gain_hbm,
    decode_project_hbm,
    decode_attr_hbm,
    decode_edge_hbm,
    out_weight_hbm,
    encode_senders_hbm,
    encode_receivers_hbm,
    encode_features_hbm,
    decode_senders_hbm,
    decode_receivers_hbm,
    decode_features_hbm,
    predicted_ref,
    gradient_ref,
    grid_in,
    target,
    mesh_in,
    embed_own,
    encode_attr_weight,
    node_gain,
    decode_attr_weight,
    out_weight,
    encode_senders,
    encode_receivers,
    encode_features,
    decode_senders,
    decode_receivers,
    decode_features,
    embed_full,
    weights_full,
    latent,
    encode_out,
    encode_in,
    decode_out,
    decode_in,
    collected,
    half_out,
    half_in,
    mine,
    pieces_out,
    pieces_in,
    final_out,
    final_in,
    load_sem,
    own_sem,
    w_send,
    w_recv,
    y_send,
    y_recv,
    f_send,
    f_recv,
    e_send,
    e_recv,
    d_send,
    d_recv,
    h_sem,
    p_send,
    p_recv,
    g_send,
    g_recv,
):
    npart, nb, nf, inside = sizes
    band, feat, rep = lax.axis_index("band"), lax.axis_index("feat"), lax.axis_index("rep")
    side = lax.axis_index("parts")
    other = 1 - rep
    width = mesh_in.shape[1]
    columns = width // nf
    values, grid_rows = grid_in.shape
    mesh_rows = mesh_in.shape[0]
    group = nb * nf
    lane = nb * 2
    shares = npart * 2

    def in_range(b):
        return jnp.logical_and(b >= 0, b < nb)

    def greet(peer):
        pl.semaphore_signal(barrier, inc=1, device_id=peer, device_id_type=MESH)

    barrier = pltpu.get_barrier_semaphore()
    for dy in range(1, npart):
        greet({"parts": lax.rem(side + dy, npart)})
    if inside:
        for db in range(nb):
            for df in range(nf):
                for dr in range(2):
                    if (db or df or dr) and not (df and dr):
                        greet(
                            {
                                "band": lax.rem(band + db, nb),
                                "feat": lax.rem(feat + df, nf),
                                "rep": lax.rem(rep + dr, 2),
                            }
                        )
    else:
        greet({"rep": other})
        for df in range(1, nf):
            greet({"feat": lax.rem(feat + df, nf)})
        for d in HOPS:
            @pl.when(in_range(band + d))
            def _():
                greet({"band": band + d})

    loads = {}
    for k, (name, src, dst) in enumerate(
        (
            ("embed", embed_hbm, embed_own),
            ("grid", grid_in_hbm, grid_in),
            ("es", encode_senders_hbm, encode_senders),
            ("ef", encode_features_hbm, encode_features),
            ("ea", encode_attr_hbm, encode_attr_weight),
            ("er", encode_receivers_hbm, encode_receivers),
            ("mesh", mesh_in_hbm, mesh_in),
            ("gain", node_gain_hbm, node_gain),
            ("ds", decode_senders_hbm, decode_senders),
            ("df", decode_features_hbm, decode_features),
            ("da", decode_attr_hbm, decode_attr_weight),
            ("dr", decode_receivers_hbm, decode_receivers),
            ("out", out_weight_hbm, out_weight),
            ("target", target_hbm, target),
        )
    ):
        loads[name] = pltpu.make_async_copy(src, dst, load_sem.at[k])
        loads[name].start()

    def loaded(*names):
        for name in names:
            loads[name].wait()

    own = pl.ds(pl.multiple_of(feat * columns, columns), columns)
    padded = embed_full.shape[0]
    shards = (
        encode_project_hbm,
        encode_edge_hbm,
        node_weight_hbm,
        decode_project_hbm,
        decode_edge_hbm,
    )
    owns = []
    for i, shard in enumerate(shards):
        owns.append(pltpu.make_async_copy(shard, weights_full.at[i, :, own], own_sem.at[i]))
        owns[i].start()
    cap_e = encode_out.shape[0] // nb
    cap_d = decode_out.shape[0] // nb
    for p in range(nb):
        @pl.when(jnp.logical_or(band - p > REACH, p - band > REACH))
        def _():
            encode_in[pl.ds(p * cap_e, cap_e), :] = jnp.zeros((cap_e, width), BF16)
            decode_in[pl.ds(p * cap_d, cap_d), :] = jnp.zeros((cap_d, width), BF16)
    base = values // 32 * 32
    embed_full[pl.ds(base, padded - base), own] = jnp.zeros((padded - base, columns), BF16)
    loaded("embed")
    embed_full[pl.ds(0, values), own] = embed_own[...]

    if inside:
        pl.semaphore_wait(barrier, npart - 1 + nb * (nf + 1) - 1)
    else:
        pl.semaphore_wait(barrier, npart - 1 + nf)
        for d in HOPS:
            @pl.when(in_range(band + d))
            def _():
                pl.semaphore_wait(barrier, 1)

    def cut(i):
        return (padded if i == 0 else width) // shares

    def spot_of(i, y, r):
        h = cut(i)
        return pl.ds(pl.multiple_of((y * 2 + r) * h, 16), h)

    def part(i, y, r, f):
        cols = pl.ds(pl.multiple_of(f * columns, columns), columns)
        if i == 0:
            return embed_full.at[spot_of(i, y, r), cols]
        return weights_full.at[i - 1, spot_of(i, y, r), cols]

    def across(i, off):
        view = part(i, side, rep, feat)
        return pltpu.make_async_remote_copy(
            src_ref=view if i == 0 else shards[i - 1].at[spot_of(i, side, rep), :],
            dst_ref=view,
            send_sem=w_send.at[i, off - 1],
            recv_sem=w_recv.at[i, off - 1],
            device_id={"feat": lax.rem(feat + off, nf)},
            device_id_type=MESH,
        )

    def traded(i, off, dy):
        view = part(i, side, rep, lax.rem(feat + nf - off, nf))
        return pltpu.make_async_remote_copy(
            src_ref=view,
            dst_ref=view,
            send_sem=y_send.at[i, off - 1, dy - 1],
            recv_sem=y_recv.at[i, off - 1, dy - 1],
            device_id={"parts": lax.rem(side + dy, npart)},
            device_id_type=MESH,
        )

    def handed(i, off, dy):
        view = part(i, lax.rem(side + npart - dy, npart), rep, lax.rem(feat + nf - off, nf))
        return pltpu.make_async_remote_copy(
            src_ref=view,
            dst_ref=view,
            send_sem=f_send.at[i, off - 1, dy],
            recv_sem=f_recv.at[i, off - 1, dy],
            device_id={"rep": other},
            device_id_type=MESH,
        )

    def hand_on(i):
        for off in range(1, nf):
            across(i, off).wait_recv()
            for dy in range(1, npart):
                traded(i, off, dy).start()
            handed(i, off, 0).start()

    def hand_over(i):
        for off in range(1, nf):
            for dy in range(1, npart):
                traded(i, off, dy).wait_recv()
                handed(i, off, dy).start()

    def ready(i):
        if i:
            owns[i - 1].wait()
        for off in range(1, nf):
            for dy in range(npart):
                handed(i, off, dy).wait_recv()

    for i in range(6):
        for off in range(1, nf):
            across(i, off).start()

    def message(out, arrive, send_sem, recv_sem, cap, k):
        return pltpu.make_async_remote_copy(
            src_ref=out.at[pl.ds(pl.multiple_of((band + HOPS[k]) * cap, cap), cap)],
            dst_ref=arrive.at[pl.ds(pl.multiple_of(band * cap, cap), cap)],
            send_sem=send_sem.at[k],
            recv_sem=recv_sem.at[k],
            device_id={"band": band + HOPS[k]},
            device_id_type=MESH,
        )

    def send_all(out, arrive, send_sem, recv_sem, cap):
        for k, d in enumerate(HOPS):
            @pl.when(in_range(band + d))
            def _():
                message(out, arrive, send_sem, recv_sem, cap, k).start()
        here = pl.ds(pl.multiple_of(band * cap, cap), cap)
        arrive[here, :] = out[here, :]

    def recv_all(out, arrive, send_sem, recv_sem, cap):
        for k, d in enumerate(HOPS):
            @pl.when(in_range(band - d))
            def _():
                pltpu.make_async_remote_copy(
                    src_ref=out.at[pl.ds(0, cap)],
                    dst_ref=arrive.at[pl.ds(pl.multiple_of((band - d) * cap, cap), cap)],
                    send_sem=send_sem.at[k],
                    recv_sem=recv_sem.at[k],
                    device_id={"band": band - d},
                    device_id_type=MESH,
                ).wait_recv()

    def sent_all(out, arrive, send_sem, recv_sem, cap):
        for k, d in enumerate(HOPS):
            @pl.when(in_range(band + d))
            def _():
                message(out, arrive, send_sem, recv_sem, cap, k).wait_send()

    enc = (encode_out, encode_in, e_send, e_recv, cap_e)
    dec = (decode_out, decode_in, d_send, d_recv, cap_d)

    def slot_row(blocks):
        return jnp.concatenate([blocks[0, pl.ds(p, 1), :] for p in range(nb)], axis=1)

    loaded("ef", "ea", "es", "grid")
    encode_attr = matmul_tn(encode_features[0], encode_attr_weight[...])
    encode_pick = onehot_rows(slot_row(encode_senders), grid_rows)
    hand_on(0)
    hand_on(1)
    hand_over(0)
    ready(0)
    latent[...] = silu(matmul_tn(grid_in[...], embed_full[pl.ds(0, values), :])).astype(BF16)
    hand_over(1)
    hand_on(2)
    ready(1)
    grid_project = matmul(latent[...], weights_full[0]).astype(BF16)
    encode_out[...] = silu(matmul_tn(encode_pick, grid_project) + encode_attr).astype(BF16)
    send_all(*enc)

    hand_over(2)
    hand_on(3)
    loaded("df", "da", "ds", "er", "dr")
    decode_attr = matmul_tn(decode_features[0], decode_attr_weight[...])
    decode_pick = onehot_rows(slot_row(decode_senders), mesh_rows)
    encode_collect = onehot_rows(slot_row(encode_receivers), mesh_rows)
    decode_collect = onehot_rows(slot_row(decode_receivers), grid_rows)
    hand_over(3)
    hand_on(4)
    recv_all(*enc)
    gathered = matmul(encode_collect, encode_in[...]).astype(BF16)
    ready(2)
    aggregated = matmul(gathered, weights_full[1]).astype(BF16)
    loaded("mesh", "gain")
    ready(3)
    update = mesh_in[...].astype(F32) + matmul(aggregated, weights_full[2])
    hand_over(4)
    hand_on(5)
    centered = update - jnp.mean(update, axis=-1, keepdims=True)
    spread = jnp.mean(centered * centered, axis=-1, keepdims=True)
    mesh_latent = (node_gain[...].astype(F32) * centered * lax.rsqrt(spread + eps_norm)).astype(BF16)
    ready(4)
    mesh_project = matmul(mesh_latent, weights_full[3]).astype(BF16)
    decode_out[...] = silu(matmul_tn(decode_pick, mesh_project) + decode_attr).astype(BF16)
    send_all(*dec)
    hand_over(5)
    loaded("out", "target")
    ready(5)
    recv_all(*dec)

    collected[...] = matmul(decode_collect, decode_in[...]).astype(BF16)
    incoming = matmul(collected[...], weights_full[4])
    decoded = (latent[...].astype(F32) + incoming).astype(BF16)
    predicted = matmul_nt(out_weight[...], decoded).astype(BF16)
    predicted_ref[...] = predicted
    scale = math.sqrt(grid_rows * nb * nf * 2)
    error = ((predicted.astype(F32) - target[...].astype(F32)) / scale).astype(BF16)
    cotangent = matmul_tn(error, out_weight[...]).astype(BF16)

    if not inside:
        gradient_ref[...] = matmul_tn(collected[...], cotangent)
    else:
        half = width // 2
        rows = half // nb

        def term(r):
            return matmul_tn(
                collected[:, pl.ds(pl.multiple_of(r * half, half), half)], cotangent
            )

        half_out[...] = term(other).astype(BF16)
        swap = pltpu.make_async_remote_copy(
            src_ref=half_out,
            dst_ref=half_in,
            send_sem=h_sem.at[0],
            recv_sem=h_sem.at[1],
            device_id={"rep": other},
            device_id_type=MESH,
        )
        swap.start()
        mine[...] = term(rep)
        swap.wait_recv()
        summed = mine[...] + half_in[...].astype(F32)
        mine[...] = summed
        pieces_out[...] = summed.astype(BF16)
        place = band * nf + feat

        def piece(k):
            to = lax.rem(place + k, group)
            tb, tf = lax.div(to, nf), lax.rem(to, nf)
            return pltpu.make_async_remote_copy(
                src_ref=pieces_out.at[
                    pl.ds(pl.multiple_of(tb * rows, 16), rows),
                    pl.ds(pl.multiple_of(tf * columns, columns), columns),
                ],
                dst_ref=pieces_in.at[k - 1],
                send_sem=p_send.at[k - 1],
                recv_sem=p_recv.at[k - 1],
                device_id={"band": tb, "feat": tf},
                device_id_type=MESH,
            )

        for k in range(1, group):
            piece(k).start()
        total = mine[pl.ds(pl.multiple_of(band * rows, 16), rows), own]
        for k in range(1, group):
            piece(k).wait_recv()
            total = total + pieces_in[k - 1].astype(F32)
        final_out[...] = total.astype(BF16)
        spot = band * 2 + rep

        def final(k):
            to = lax.rem(spot + k, lane)
            return pltpu.make_async_remote_copy(
                src_ref=final_out,
                dst_ref=final_in.at[k - 1],
                send_sem=g_send.at[k - 1],
                recv_sem=g_recv.at[k - 1],
                device_id={"band": lax.div(to, 2), "rep": lax.rem(to, 2)},
                device_id_type=MESH,
            )

        def rows_of(s):
            start = lax.rem(s, 2) * half + lax.div(s, 2) * rows
            return pl.ds(pl.multiple_of(start, 16), rows)

        for k in range(1, lane):
            final(k).start()
        gradient_ref[rows_of(spot), :] = final_out[...]
        for k in range(1, lane):
            final(k).wait_recv()
            gradient_ref[rows_of(lax.rem(spot + lane - k, lane)), :] = final_in[k - 1]

    for i in range(6):
        for off in range(1, nf):
            across(i, off).wait_send()
            for dy in range(npart):
                handed(i, off, dy).wait_send()
            for dy in range(1, npart):
                traded(i, off, dy).wait_send()
    sent_all(*enc)
    sent_all(*dec)
    if inside:
        swap.wait_send()
        for k in range(1, group):
            piece(k).wait_send()
        for k in range(1, lane):
            final(k).wait_send()


def local(sizes, *args):
    npart, nb, nf, inside = sizes
    args = list(args)
    mesh_in = args[2]
    for at in (0, 1, 12):
        args[at] = args[at].T
    values, grid_rows = args[0].shape
    width = mesh_in.shape[1]
    columns = width // nf
    args[8] = args[8].reshape(1, width)
    cap_e = math.prod(args[13].shape)
    cap_d = math.prod(args[16].shape)
    half = width // 2
    rows = half // nb if inside else 16
    padded = -(-values // (32 * npart)) * 32 * npart
    slots = max(nf - 1, 1)
    trades = max(npart - 1, 1)
    dma = pltpu.SemaphoreType.DMA
    group, lane = (nb * nf, nb * 2) if inside else (2, 2)
    held = (0, 1, 2, 3, 5, 8, 10, 12, 13, 14, 15, 16, 17, 18)
    predicted, gradient = pl.pallas_call(
        functools.partial(forecaster, sizes),
        out_shape=(
            jax.ShapeDtypeStruct((values, grid_rows), BF16),
            jax.ShapeDtypeStruct(
                (width, columns if inside else width), BF16 if inside else F32
            ),
        ),
        in_specs=[pl.BlockSpec(memory_space=pltpu.HBM)] * len(args),
        out_specs=(pl.BlockSpec(memory_space=pltpu.VMEM),) * 2,
        scratch_shapes=[pltpu.VMEM(args[at].shape, args[at].dtype) for at in held]
        + [
            pltpu.VMEM((padded, width), BF16),
            pltpu.VMEM((5, width, width), BF16),
            pltpu.VMEM((grid_rows, width), BF16),
            pltpu.VMEM((cap_e, width), BF16),
            pltpu.VMEM((cap_e, width), BF16),
            pltpu.VMEM((cap_d, width), BF16),
            pltpu.VMEM((cap_d, width), BF16),
            pltpu.VMEM((grid_rows, width), BF16),
            pltpu.VMEM((half, width), BF16),
            pltpu.VMEM((half, width), BF16),
            pltpu.VMEM((half, width), F32),
            pltpu.VMEM((half, width), BF16),
            pltpu.VMEM((group - 1, rows, columns), BF16),
            pltpu.VMEM((rows, columns), BF16),
            pltpu.VMEM((lane - 1, rows, columns), BF16),
            dma((len(held),)),
            dma((5,)),
            dma((6, slots)),
            dma((6, slots)),
            dma((6, slots, trades)),
            dma((6, slots, trades)),
            dma((6, slots, npart)),
            dma((6, slots, npart)),
            dma((len(HOPS),)),
            dma((len(HOPS),)),
            dma((len(HOPS),)),
            dma((len(HOPS),)),
            dma((2,)),
            dma((group - 1,)),
            dma((group - 1,)),
            dma((lane - 1,)),
            dma((lane - 1,)),
        ],
        compiler_params=pltpu.CompilerParams(
            collective_id=0, has_side_effects=True, vmem_limit_bytes=48 * 1024 * 1024
        ),
    )(*args)
    if inside:
        gradient = gradient.astype(F32)
    else:
        total = lax.psum(gradient, ("band", "feat", "rep"))
        gradient = lax.dynamic_slice_in_dim(total, lax.axis_index("feat") * columns, columns, 1)
    return (predicted.T, gradient)


def solution(mesh):
    npart, nb, nf = mesh.shape["parts"], mesh.shape["band"], mesh.shape["feat"]
    inside = nb <= 8 and nf <= 2
    slab = ("parts", "band", "feat", "rep")
    return jax.shard_map(
        functools.partial(local, (npart, nb, nf, inside)),
        mesh=mesh,
        in_specs=(
            P(slab, None),
            P(slab, None),
            P(slab, None),
            P(None, "feat"),
            P(None, "feat"),
            P(),
            P(None, "feat"),
            P(None, "feat"),
            P(),
            P(None, "feat"),
            P(),
            P(None, "feat"),
            P(),
        )
        + (P(slab, None, None),) * 6,
        out_specs=(P(slab, None), P("parts", "feat")),
        check_vma=False,
    )
```

```python
import functools
import math

import jax
import jax.numpy as jnp
from jax import lax
from jax.experimental import pallas as pl
from jax.experimental.pallas import tpu as pltpu
from jax.sharding import PartitionSpec as P

eps_norm = 1e-05
MESH = pl.DeviceIdType.MESH
F32 = jnp.float32
BF16 = jnp.bfloat16
REACH = 2
HOPS = tuple(d for d in range(-REACH, REACH + 1) if d != 0)


def silu(v):
    return v / (1.0 + jnp.exp(-v))


def matmul(a, b):
    return jnp.dot(a, b, preferred_element_type=F32)


def matmul_tn(a, b):
    return lax.dot_general(a, b, (((0,), (0,)), ((), ())), preferred_element_type=F32)


def matmul_nt(a, b):
    return lax.dot_general(a, b, (((1,), (1,)), ((), ())), preferred_element_type=F32)


def onehot_rows(index_row, rows):
    at = lax.broadcasted_iota(jnp.int32, (rows, index_row.shape[1]), 0)
    return jnp.where(at == index_row, 1.0, 0.0).astype(BF16)


def forecaster(
    sizes,
    grid_in_hbm,
    target_hbm,
    mesh_in_hbm,
    embed_hbm,
    encode_project_hbm,
    encode_attr_hbm,
    encode_edge_hbm,
    node_weight_hbm,
    node_gain_hbm,
    decode_project_hbm,
    decode_attr_hbm,
    decode_edge_hbm,
    out_weight_hbm,
    encode_senders_hbm,
    encode_receivers_hbm,
    encode_features_hbm,
    decode_senders_hbm,
    decode_receivers_hbm,
    decode_features_hbm,
    predicted_ref,
    gradient_ref,
    grid_in,
    target,
    mesh_in,
    embed_own,
    encode_attr_weight,
    node_gain,
    decode_attr_weight,
    out_weight,
    encode_senders,
    encode_receivers,
    encode_features,
    decode_senders,
    decode_receivers,
    decode_features,
    embed_full,
    weights_full,
    latent,
    encode_out,
    encode_in,
    decode_out,
    decode_in,
    collected,
    half_out,
    half_in,
    mine,
    pieces_out,
    pieces_in,
    final_out,
    final_in,
    load_sem,
    own_sem,
    w_send,
    w_recv,
    y_send,
    y_recv,
    f_send,
    f_recv,
    e_send,
    e_recv,
    d_send,
    d_recv,
    h_sem,
    p_send,
    p_recv,
    g_send,
    g_recv,
):
    npart, nb, nf, inside = sizes
    band, feat, rep = lax.axis_index("band"), lax.axis_index("feat"), lax.axis_index("rep")
    side = lax.axis_index("parts") if npart > 1 else 0
    other = 1 - rep
    width = mesh_in.shape[1]
    columns = width // nf
    values, grid_rows = grid_in.shape
    mesh_rows = mesh_in.shape[0]
    group = nb * nf
    shares = npart * 2

    def in_range(b):
        return jnp.logical_and(b >= 0, b < nb)

    def greet(peer):
        pl.semaphore_signal(barrier, inc=1, device_id=peer, device_id_type=MESH)

    barrier = pltpu.get_barrier_semaphore()
    for dy in range(1, npart):
        greet({"parts": lax.rem(side + dy, npart)})
    if inside:
        greet({"rep": other})
        for db in range(nb):
            for df in range(nf):
                if db or df:
                    greet({"band": lax.rem(band + db, nb), "feat": lax.rem(feat + df, nf)})
    else:
        greet({"rep": other})
        for df in range(1, nf):
            greet({"feat": lax.rem(feat + df, nf)})
        for d in HOPS:
            @pl.when(in_range(band + d))
            def _():
                greet({"band": band + d})

    loads = {}
    for k, (name, src, dst) in enumerate(
        (
            ("embed", embed_hbm, embed_own),
            ("grid", grid_in_hbm, grid_in),
            ("es", encode_senders_hbm, encode_senders),
            ("ef", encode_features_hbm, encode_features),
            ("ea", encode_attr_hbm, encode_attr_weight),
            ("er", encode_receivers_hbm, encode_receivers),
            ("mesh", mesh_in_hbm, mesh_in),
            ("gain", node_gain_hbm, node_gain),
            ("ds", decode_senders_hbm, decode_senders),
            ("df", decode_features_hbm, decode_features),
            ("da", decode_attr_hbm, decode_attr_weight),
            ("dr", decode_receivers_hbm, decode_receivers),
            ("out", out_weight_hbm, out_weight),
            ("target", target_hbm, target),
        )
    ):
        loads[name] = pltpu.make_async_copy(src, dst, load_sem.at[k])
        loads[name].start()

    def loaded(*names):
        for name in names:
            loads[name].wait()

    own = pl.ds(pl.multiple_of(feat * columns, columns), columns)
    padded = embed_full.shape[1]
    shards = (
        encode_project_hbm,
        encode_edge_hbm,
        node_weight_hbm,
        decode_project_hbm,
        decode_edge_hbm,
    )
    owns = []
    for i, shard in enumerate(shards):
        owns.append(pltpu.make_async_copy(shard, weights_full.at[i, feat], own_sem.at[i]))
        owns[i].start()
    cap_e = encode_out.shape[0] // nb
    cap_d = decode_out.shape[0] // nb
    for p in range(nb):
        @pl.when(jnp.logical_or(band - p > REACH, p - band > REACH))
        def _():
            encode_in[pl.ds(p * cap_e, cap_e), :] = jnp.zeros((cap_e, width), BF16)
            decode_in[pl.ds(p * cap_d, cap_d), :] = jnp.zeros((cap_d, width), BF16)
    base = values // 32 * 32
    embed_full[feat, pl.ds(base, padded - base), :] = jnp.zeros((padded - base, columns), BF16)
    loaded("embed")
    embed_full[feat, pl.ds(0, values), :] = embed_own[...]

    if inside:
        pl.semaphore_wait(barrier, npart - 1 + group)
    else:
        pl.semaphore_wait(barrier, npart - 1 + nf)
        for d in HOPS:
            @pl.when(in_range(band + d))
            def _():
                pl.semaphore_wait(barrier, 1)

    def cut(i):
        return (padded if i == 0 else width) // shares

    def spot_of(i, y, r):
        h = cut(i)
        return pl.ds(pl.multiple_of((y * 2 + r) * h, 16), h)

    def part(i, y, r, f):
        if i == 0:
            return embed_full.at[f, spot_of(i, y, r), :]
        return weights_full.at[i - 1, f, spot_of(i, y, r), :]

    def across(i, off):
        view = part(i, side, rep, feat)
        return pltpu.make_async_remote_copy(
            src_ref=view if i == 0 else shards[i - 1].at[spot_of(i, side, rep), :],
            dst_ref=view,
            send_sem=w_send.at[i, off - 1],
            recv_sem=w_recv.at[i, off - 1],
            device_id={"feat": lax.rem(feat + off, nf)},
            device_id_type=MESH,
        )

    def traded(i, off, dy):
        view = part(i, side, rep, lax.rem(feat + nf - off, nf))
        return pltpu.make_async_remote_copy(
            src_ref=view,
            dst_ref=view,
            send_sem=y_send.at[i, off - 1, dy - 1],
            recv_sem=y_recv.at[i, off - 1, dy - 1],
            device_id={"parts": lax.rem(side + dy, npart)},
            device_id_type=MESH,
        )

    def handed(i, off, dy):
        view = part(i, lax.rem(side + npart - dy, npart), rep, lax.rem(feat + nf - off, nf))
        return pltpu.make_async_remote_copy(
            src_ref=view,
            dst_ref=view,
            send_sem=f_send.at[i, off - 1, dy],
            recv_sem=f_recv.at[i, off - 1, dy],
            device_id={"rep": other},
            device_id_type=MESH,
        )

    def hand_on(i):
        for off in range(1, nf):
            across(i, off).wait_recv()
            for dy in range(1, npart):
                traded(i, off, dy).start()
            handed(i, off, 0).start()

    def hand_over(i):
        for off in range(1, nf):
            for dy in range(1, npart):
                traded(i, off, dy).wait_recv()
                handed(i, off, dy).start()

    def ready(i):
        if i:
            owns[i - 1].wait()
        for off in range(1, nf):
            for dy in range(npart):
                handed(i, off, dy).wait_recv()

    for i in range(6):
        for off in range(1, nf):
            across(i, off).start()

    def message(out, arrive, send_sem, recv_sem, cap, k):
        return pltpu.make_async_remote_copy(
            src_ref=out.at[pl.ds(pl.multiple_of((band + HOPS[k]) * cap, cap), cap)],
            dst_ref=arrive.at[pl.ds(pl.multiple_of(band * cap, cap), cap)],
            send_sem=send_sem.at[k],
            recv_sem=recv_sem.at[k],
            device_id={"band": band + HOPS[k]},
            device_id_type=MESH,
        )

    def send_all(out, arrive, send_sem, recv_sem, cap):
        for k, d in enumerate(HOPS):
            @pl.when(in_range(band + d))
            def _():
                message(out, arrive, send_sem, recv_sem, cap, k).start()
        here = pl.ds(pl.multiple_of(band * cap, cap), cap)
        arrive[here, :] = out[here, :]

    def recv_all(out, arrive, send_sem, recv_sem, cap):
        for k, d in enumerate(HOPS):
            @pl.when(in_range(band - d))
            def _():
                pltpu.make_async_remote_copy(
                    src_ref=out.at[pl.ds(0, cap)],
                    dst_ref=arrive.at[pl.ds(pl.multiple_of((band - d) * cap, cap), cap)],
                    send_sem=send_sem.at[k],
                    recv_sem=recv_sem.at[k],
                    device_id={"band": band - d},
                    device_id_type=MESH,
                ).wait_recv()

    def sent_all(out, arrive, send_sem, recv_sem, cap):
        for k, d in enumerate(HOPS):
            @pl.when(in_range(band + d))
            def _():
                message(out, arrive, send_sem, recv_sem, cap, k).wait_send()

    enc = (encode_out, encode_in, e_send, e_recv, cap_e)
    dec = (decode_out, decode_in, d_send, d_recv, cap_d)

    def weigh(activation, i):
        return jnp.concatenate([matmul(activation, weights_full[i, f]) for f in range(nf)], axis=1)

    def slot_row(blocks):
        return jnp.concatenate([blocks[0, pl.ds(p, 1), :] for p in range(nb)], axis=1)

    loaded("ef", "ea", "es", "grid")
    encode_attr = matmul_tn(encode_features[0], encode_attr_weight[...])
    encode_pick = onehot_rows(slot_row(encode_senders), grid_rows)
    hand_on(0)
    hand_on(1)
    hand_over(0)
    ready(0)
    latent[...] = silu(
        jnp.concatenate(
            [matmul_tn(grid_in[...], embed_full[f, pl.ds(0, values), :]) for f in range(nf)], axis=1
        )
    ).astype(BF16)
    hand_over(1)
    hand_on(2)
    ready(1)
    grid_project = weigh(latent[...], 0).astype(BF16)
    encode_out[...] = silu(matmul_tn(encode_pick, grid_project) + encode_attr).astype(BF16)
    send_all(*enc)

    hand_over(2)
    hand_on(3)
    loaded("df", "da", "ds", "er", "dr")
    decode_attr = matmul_tn(decode_features[0], decode_attr_weight[...])
    decode_pick = onehot_rows(slot_row(decode_senders), mesh_rows)
    encode_collect = onehot_rows(slot_row(encode_receivers), mesh_rows)
    decode_collect = onehot_rows(slot_row(decode_receivers), grid_rows)
    hand_over(3)
    hand_on(4)
    recv_all(*enc)
    gathered = matmul(encode_collect, encode_in[...]).astype(BF16)
    ready(2)
    aggregated = weigh(gathered, 1).astype(BF16)
    loaded("mesh", "gain")
    ready(3)
    update = mesh_in[...].astype(F32) + weigh(aggregated, 2)
    hand_over(4)
    hand_on(5)
    centered = update - jnp.mean(update, axis=-1, keepdims=True)
    spread = jnp.mean(centered * centered, axis=-1, keepdims=True)
    mesh_latent = (node_gain[...].astype(F32).reshape(1, width) * centered * lax.rsqrt(spread + eps_norm)).astype(BF16)
    ready(4)
    mesh_project = weigh(mesh_latent, 3).astype(BF16)
    decode_out[...] = silu(matmul_tn(decode_pick, mesh_project) + decode_attr).astype(BF16)
    send_all(*dec)
    hand_over(5)
    loaded("out", "target")
    ready(5)
    recv_all(*dec)

    collected[...] = matmul(decode_collect, decode_in[...]).astype(BF16)
    incoming = weigh(collected[...], 4)
    decoded = (latent[...].astype(F32) + incoming).astype(BF16)
    predicted = matmul_nt(out_weight[...], decoded).astype(BF16)
    predicted_ref[...] = predicted
    scale = math.sqrt(grid_rows * nb * nf * 2)
    error = ((predicted.astype(F32) - target[...].astype(F32)) / scale).astype(BF16)
    cotangent = matmul_tn(error, out_weight[...]).astype(BF16)

    if not inside:
        gradient_ref[...] = matmul_tn(collected[...], cotangent)
    else:
        half = width // 2
        rows = half // nb

        def term(r):
            return matmul_tn(
                collected[:, pl.ds(pl.multiple_of(r * half, half), half)], cotangent
            )

        half_out[...] = term(other).astype(BF16)
        swap = pltpu.make_async_remote_copy(
            src_ref=half_out,
            dst_ref=half_in,
            send_sem=h_sem.at[0],
            recv_sem=h_sem.at[1],
            device_id={"rep": other},
            device_id_type=MESH,
        )
        swap.start()
        mine[...] = term(rep)
        swap.wait_recv()
        summed = mine[...] + half_in[...].astype(F32)
        mine[...] = summed
        pieces_out[...] = summed.astype(BF16)
        place = band * nf + feat

        def piece(k):
            to = lax.rem(place + k, group)
            tb, tf = lax.div(to, nf), lax.rem(to, nf)
            return pltpu.make_async_remote_copy(
                src_ref=pieces_out.at[
                    pl.ds(pl.multiple_of(tb * rows, 16), rows),
                    pl.ds(pl.multiple_of(tf * columns, columns), columns),
                ],
                dst_ref=pieces_in.at[k - 1],
                send_sem=p_send.at[k - 1],
                recv_sem=p_recv.at[k - 1],
                device_id={"band": tb, "feat": tf},
                device_id_type=MESH,
            )

        for k in range(1, group):
            piece(k).start()
        total = mine[pl.ds(pl.multiple_of(band * rows, 16), rows), own]
        for k in range(1, group):
            piece(k).wait_recv()
            total = total + pieces_in[k - 1].astype(F32)
        final_out[...] = total.astype(BF16)

        def around(k):
            return pltpu.make_async_remote_copy(
                src_ref=final_out,
                dst_ref=final_in.at[k - 1],
                send_sem=g_send.at[k - 1],
                recv_sem=g_recv.at[k - 1],
                device_id={"band": lax.rem(band + k, nb)},
                device_id_type=MESH,
            )

        def beside(k):
            return pltpu.make_async_remote_copy(
                src_ref=final_in.at[k - 1] if k else final_out,
                dst_ref=final_in.at[nb - 1 + k],
                send_sem=g_send.at[nb - 1 + k],
                recv_sem=g_recv.at[nb - 1 + k],
                device_id={"rep": other},
                device_id_type=MESH,
            )

        def rows_of(r, k):
            start = r * half + lax.rem(band + nb - k, nb) * rows
            return pl.ds(pl.multiple_of(start, 16), rows)

        for k in range(1, nb):
            around(k).start()
        beside(0).start()
        gradient_ref[rows_of(rep, 0), :] = final_out[...].astype(F32)
        for k in range(1, nb):
            around(k).wait_recv()
            beside(k).start()
            gradient_ref[rows_of(rep, k), :] = final_in[k - 1].astype(F32)
        for k in range(nb):
            beside(k).wait_recv()
            gradient_ref[rows_of(other, k), :] = final_in[nb - 1 + k].astype(F32)

    for i in range(6):
        for off in range(1, nf):
            across(i, off).wait_send()
            for dy in range(npart):
                handed(i, off, dy).wait_send()
            for dy in range(1, npart):
                traded(i, off, dy).wait_send()
    sent_all(*enc)
    sent_all(*dec)
    if inside:
        swap.wait_send()
        for k in range(1, group):
            piece(k).wait_send()
        for k in range(1, nb):
            around(k).wait_send()
        for k in range(nb):
            beside(k).wait_send()


def local(sizes, *args):
    npart, nb, nf, inside = sizes
    args = list(args)
    mesh_in = args[2]
    for at in (0, 1, 12):
        args[at] = args[at].T
    values, grid_rows = args[0].shape
    width = mesh_in.shape[1]
    columns = width // nf
    cap_e = math.prod(args[13].shape)
    cap_d = math.prod(args[16].shape)
    half = width // 2
    rows = half // nb if inside else 16
    padded = -(-values // (32 * npart)) * 32 * npart
    slots = max(nf - 1, 1)
    trades = max(npart - 1, 1)
    dma = pltpu.SemaphoreType.DMA
    group, lane = (nb * nf, nb * 2) if inside else (2, 2)
    held = (0, 1, 2, 3, 5, 8, 10, 12, 13, 14, 15, 16, 17, 18)
    predicted, gradient = pl.pallas_call(
        functools.partial(forecaster, sizes),
        out_shape=(
            jax.ShapeDtypeStruct((values, grid_rows), BF16),
            jax.ShapeDtypeStruct((width, columns if inside else width), F32),
        ),
        in_specs=[pl.BlockSpec(memory_space=pl.ANY)] * len(args),
        out_specs=(pl.BlockSpec(memory_space=pltpu.VMEM),) * 2,
        scratch_shapes=[pltpu.VMEM(args[at].shape, args[at].dtype) for at in held]
        + [
            pltpu.VMEM((nf, padded, columns), BF16),
            pltpu.VMEM((5, nf, width, columns), BF16),
            pltpu.VMEM((grid_rows, width), BF16),
            pltpu.VMEM((cap_e, width), BF16),
            pltpu.VMEM((cap_e, width), BF16),
            pltpu.VMEM((cap_d, width), BF16),
            pltpu.VMEM((cap_d, width), BF16),
            pltpu.VMEM((grid_rows, width), BF16),
            pltpu.VMEM((half, width), BF16),
            pltpu.VMEM((half, width), BF16),
            pltpu.VMEM((half, width), F32),
            pltpu.VMEM((half, width), BF16),
            pltpu.VMEM((group - 1, rows, columns), BF16),
            pltpu.VMEM((rows, columns), BF16),
            pltpu.VMEM((lane - 1, rows, columns), BF16),
            dma((len(held),)),
            dma((5,)),
            dma((6, slots)),
            dma((6, slots)),
            dma((6, slots, trades)),
            dma((6, slots, trades)),
            dma((6, slots, npart)),
            dma((6, slots, npart)),
            dma((len(HOPS),)),
            dma((len(HOPS),)),
            dma((len(HOPS),)),
            dma((len(HOPS),)),
            dma((2,)),
            dma((group - 1,)),
            dma((group - 1,)),
            dma((lane - 1,)),
            dma((lane - 1,)),
        ],
        compiler_params=pltpu.CompilerParams(
            collective_id=0, has_side_effects=True, vmem_limit_bytes=63 * 1024 * 1024
        ),
    )(*args)
    if not inside:
        total = lax.psum(gradient, ("band", "feat", "rep"))
        gradient = lax.dynamic_slice_in_dim(total, lax.axis_index("feat") * columns, columns, 1)
    return (predicted.T, gradient)


def solution(mesh):
    npart, nb, nf = 1, mesh.shape["band"], mesh.shape["feat"]
    inside = nb <= 8 and nf <= 2
    slab = ("parts", "band", "feat", "rep")
    return jax.shard_map(
        functools.partial(local, (npart, nb, nf, inside)),
        mesh=mesh,
        in_specs=(
            P(slab, None),
            P(slab, None),
            P(slab, None),
            P(None, "feat"),
            P(None, "feat"),
            P(),
            P(None, "feat"),
            P(None, "feat"),
            P(),
            P(None, "feat"),
            P(),
            P(None, "feat"),
            P(),
        )
        + (P(slab, None, None),) * 6,
        out_specs=(P(slab, None), P("parts", "feat")),
        check_vma=False,
    )
```
